32 devices in a mesh: lat: 8 (over y, x, core), lon: 4 (over z).
Axes of the slice: x: 2, y: 2, z: 4, core: 2. Of those that a mesh axis runs over, the one named last changes fastest.
Arguments:
- current_sample: float32 [4, 256, 1024], P(None, 'lat', 'lon'), may hold values from -6 to 6
- churn_noise: float32 [4, 256, 1024], P(None, 'lat', 'lon'), may hold values from -6 to 6
- coarse_fields: float32 [12, 32, 128], P(None, 'lat', 'lon'), may hold values from -6 to 6
- tile_owner: int32 [8], replicated, may hold values from 0 to 7, each once
- input_kernel: bfloat16 [3, 3, 16, 128], replicated, may hold values from -0.5 to 0.5
- fine_first: bfloat16 [3, 3, 128, 128], replicated, may hold values from -0.1875 to 0.1875
- fine_second: bfloat16 [3, 3, 128, 128], replicated, may hold values from -0.1875 to 0.1875
- coarse_first: bfloat16 [3, 3, 128, 128], replicated, may hold values from -0.1875 to 0.1875
- coarse_second: bfloat16 [3, 3, 128, 128], replicated, may hold values from -0.1875 to 0.1875
- output_kernel: bfloat16 [3, 3, 128, 4], replicated, may hold values from -0.5 to 0.5
Outputs:
- next_sample: float32 [4, 256, 1024], P(None, 'lat', 'lon')
The draws below stay inside these ranges and needn't reach their ends.
Inputs may be any that keep to these rules, and one draw needn't show every extreme that they name: `tile_owner`: each value is the row block's position along the bands; every stored block covers exactly one band.
All inputs are finite; a program needn't handle non-finite values.
Results may differ from the reference program's by a relative error of at most 0.0055.
Values may be sent and summed in bfloat16 or wider, within the bound.
A program may use at most 64 MiB of HBM per device.

```python
import math
import jax
import jax.numpy as jnp
from jax import lax

CH = 128
VARS = 4
CVARS = 12
RATIO = 8
NLAT = 256
NLON = 1024
BANDS = 8


def block_levels(key, extent, split, smallest, largest):
    def one(position, blocks):
        draws = jax.random.uniform(jax.random.fold_in(jax.random.fold_in(key, 6), position), (blocks,), jnp.float32, smallest / len(split), largest / len(split))
        return jnp.repeat(jnp.exp(draws), extent[position] // blocks).reshape((-1,) + (1,) * (len(extent) - position - 1))

    level = one(*split[0])
    for cut in split[1:]:
        level = level * one(*cut)
    return level


def centred(stream_key, dims, spread, most, split=(), held_as=jnp.bfloat16):
    array = spread * jax.random.normal(stream_key, dims, jnp.float32)
    if split:
        array = array * block_levels(stream_key, dims, split, -0.22, 0.18)
    return jnp.clip(array, -most, most).astype(held_as)


def setup_inputs(seed: int = 0) -> dict:
    streams_of = jax.random.split(jax.random.key(seed), 11)
    current_sample = centred(streams_of[0], (VARS, NLAT, NLON), 1.0, 6.0, ((1, 8), (2, 4)), jnp.float32)
    churn_noise = centred(streams_of[1], (VARS, NLAT, NLON), 1.0, 6.0, ((1, 8), (2, 4)), jnp.float32)
    coarse_fields = centred(streams_of[2], (CVARS, NLAT // RATIO, NLON // RATIO), 1.0, 6.0, ((1, 8), (2, 4)), jnp.float32)
    tile_owner = jax.random.permutation(streams_of[3], BANDS).astype(jnp.int32)
    input_kernel = centred(streams_of[4], (3, 3, VARS + CVARS, CH), (9 * (VARS + CVARS)) ** -0.5, 0.5)
    fine_first = centred(streams_of[5], (3, 3, CH, CH), (9 * CH) ** -0.5, 0.1875)
    fine_second = centred(streams_of[6], (3, 3, CH, CH), (9 * CH) ** -0.5, 0.1875)
    coarse_first = centred(streams_of[7], (3, 3, CH, CH), (9 * CH) ** -0.5, 0.1875)
    coarse_second = centred(streams_of[8], (3, 3, CH, CH), (9 * CH) ** -0.5, 0.1875)
    output_kernel = centred(streams_of[9], (3, 3, CH, VARS), CH ** -0.5, 0.5)
    return {"current_sample": current_sample, "churn_noise": churn_noise, "coarse_fields": coarse_fields, "tile_owner": tile_owner, "input_kernel": input_kernel, "fine_first": fine_first, "fine_second": fine_second, "coarse_first": coarse_first, "coarse_second": coarse_second, "output_kernel": output_kernel}


sigma_now = 1.0
sigma_hat = 1.2
sigma_next = 0.4
sigma_data = 0.5

def sphere_pad(values):
    half = values.shape[2] // 2
    north_rows = jnp.roll(values[:, :1, :], -half, axis=2)
    south_rows = jnp.roll(values[:, -1:, :], -half, axis=2)
    with_rows = jnp.concatenate([north_rows, values, south_rows], axis=1)
    return jnp.concatenate([with_rows[:, :, -1:], with_rows, with_rows[:, :, :1]], axis=2)

def convolve(values, kernel):
    padded = sphere_pad(values).astype(jnp.float32)[None]
    result = lax.conv_general_dilated(padded, kernel.astype(jnp.float32), (1, 1), 'VALID', dimension_numbers=('NCHW', 'HWIO', 'NCHW'), precision=lax.Precision.HIGHEST)
    return result[0]

def silu_round(values):
    return jax.nn.silu(values.astype(jnp.float32)).astype(jnp.bfloat16)

def reference(current_sample, churn_noise, coarse_fields, tile_owner, input_kernel, fine_first, fine_second, coarse_first, coarse_second, output_kernel):
    band_count = tile_owner.shape[0]
    block_rows = coarse_fields.shape[1] // band_count
    blocks = coarse_fields.reshape(coarse_fields.shape[0], band_count, block_rows, coarse_fields.shape[2])
    condition = jnp.take(blocks, tile_owner, axis=1).reshape(coarse_fields.shape)
    condition = jnp.repeat(jnp.repeat(condition, RATIO, axis=1), RATIO, axis=2)
    perturbed = current_sample + math.sqrt(sigma_hat ** 2 - sigma_now ** 2) * churn_noise
    scale_in = 1.0 / math.sqrt(sigma_hat ** 2 + sigma_data ** 2)
    net_in = jnp.concatenate([perturbed * scale_in, condition], axis=0).astype(jnp.bfloat16)
    stem = convolve(net_in, input_kernel).astype(jnp.bfloat16)
    fine_act = silu_round(stem)
    fine_hidden = silu_round(convolve(fine_act, fine_first))
    fine_out = ((stem.astype(jnp.float32) + convolve(fine_hidden, fine_second)) * math.sqrt(0.5)).astype(jnp.bfloat16)
    channels, lat_rows, lon_cols = fine_out.shape
    pooled = fine_out.astype(jnp.float32).reshape(channels, lat_rows // 2, 2, lon_cols // 2, 2).mean(axis=(2, 4)).astype(jnp.bfloat16)
    coarse_act = silu_round(pooled)
    coarse_hidden = silu_round(convolve(coarse_act, coarse_first))
    coarse_out = ((pooled.astype(jnp.float32) + convolve(coarse_hidden, coarse_second)) * math.sqrt(0.5)).astype(jnp.bfloat16)
    widened = jnp.repeat(jnp.repeat(coarse_out, 2, axis=1), 2, axis=2)
    merged = silu_round((fine_out.astype(jnp.float32) + widened.astype(jnp.float32)) * math.sqrt(0.5))
    network = convolve(merged, output_kernel)
    denom = sigma_hat ** 2 + sigma_data ** 2
    denoised = sigma_data ** 2 / denom * perturbed + sigma_hat * sigma_data / math.sqrt(denom) * network
    return perturbed + (sigma_next - sigma_hat) / sigma_hat * (perturbed - denoised)
```

```python
import functools
import math

import jax
import jax.numpy as jnp
from jax import lax
from jax.experimental import pallas as pl
from jax.experimental.pallas import tpu as pltpu
from jax.sharding import PartitionSpec as P

RATIO = 8
Q = 16
COL_HALO = 16
OUT_HALO = 6
ROW_HALO = OUT_HALO + 3
CELL_HALO = 2

sigma_now = 1.0
sigma_hat = 1.2
sigma_next = 0.4
sigma_data = 0.5
half_root = math.sqrt(0.5)
f32 = jnp.float32
bf16 = jnp.bfloat16


def silu(v):
    h = 0.5 * v
    return h + h * jnp.tanh(h)


def put_row(ref, row, value, span):
    channels = value.shape[-1]
    value = value.reshape(span, Q, channels)
    ref[row, pl.ds(1, span)] = value.astype(bf16)
    ref[row, 0] = pltpu.roll(value[span - 1], 1, 0).astype(bf16)
    ref[row, span + 1] = pltpu.roll(value[0], Q - 1, 0).astype(bf16)


def conv_pair(src, row, forward, weights, span):
    channels = src.shape[-1]
    parts = []
    for k in range(4):
        at = jnp.where(forward, row + k, row + 3 - k)
        for b in range(3):
            parts.append(src[at, pl.ds(b, span)].reshape(span * Q, channels))
    return jnp.dot(jnp.concatenate(parts, axis=1), weights[...], preferred_element_type=f32)


def kernel(
    north, south, halves_ref, ext_ref, cell_ref, pert_ref, stem_w, first_w, second_w, cfirst_w, csecond_w, out_w,
    res_ref, net, stem, act, hidden, fine, pooled, cact, chidden, cout, terms, rows_out,
):
    del halves_ref
    variables, rows, width = pert_ref.shape
    channels = stem.shape[-1]
    span = stem.shape[1]
    half_span = span // 2
    pixels = span * Q
    lanes = net.shape[-1]
    ext_cols = ext_ref.shape[1]
    ext_rows = rows + 2 * ROW_HALO

    def onehot(depth, cell):
        at = lax.broadcasted_iota(jnp.int32, (depth, lanes), 0)
        lane = lax.broadcasted_iota(jnp.int32, (depth, lanes), 1)
        column = (lane % Q) * span + lane // Q - 1
        inside = (column >= 0) & (column < ext_cols) & (lane < (span + 2) * Q)
        return jnp.where(inside & (at == column // cell), 1.0, 0.0).astype(bf16)

    fine_cols = jnp.dot(ext_ref[...], onehot(ext_cols, 1), preferred_element_type=f32)
    cell_cols = jnp.dot(cell_ref[...], onehot(cell_ref.shape[1], RATIO), preferred_element_type=f32)
    for r in range(ext_rows):
        cell = (r - ROW_HALO + CELL_HALO * RATIO) // RATIO
        both = fine_cols[r * 16 : r * 16 + 16] + cell_cols[cell * 16 : cell * 16 + 16]
        for b in range(3):
            moved = both if b == 0 else pltpu.roll(both, lanes - b * Q, 1)
            net[r, pl.ds(b * 16, 16)] = moved.astype(bf16)

    def regions(halo_pairs, pairs, body):
        def step(i, carry):
            mirrored = (north & (i < halo_pairs)) | (south & (i >= halo_pairs + pairs))
            body(i, jnp.logical_not(mirrored))
            return carry

        lax.fori_loop(0, 2 * halo_pairs + pairs, step, 0)

    def order(row, forward):
        return jnp.where(forward, row, row + 1), jnp.where(forward, row + 1, row)

    stem_halo = ROW_HALO - 1

    def stem_step(i, forward):
        parts = [net[jnp.where(forward, 2 * i + k, 2 * i + 3 - k)][:, :pixels] for k in range(4)]
        both = lax.dot_general(
            jnp.concatenate(parts, axis=0), stem_w[...], (((0,), (0,)), ((), ())), preferred_element_type=f32
        )
        for p, at in enumerate(order(2 * i, forward)):
            value = both[:, p * channels : (p + 1) * channels].astype(bf16)
            stem[at] = value.reshape(span, Q, channels)
            put_row(act, at + 1, silu(value.astype(f32)), span)

    act[0] = jnp.zeros(act.shape[1:], bf16)
    act[ext_rows - 1] = jnp.zeros(act.shape[1:], bf16)
    regions(stem_halo // 2, rows // 2, stem_step)

    def first_step(i, forward):
        both = conv_pair(act, 2 * i, forward, first_w, span)
        for p, at in enumerate(order(2 * i, forward)):
            put_row(hidden, at, silu(both[:, p * channels : (p + 1) * channels]), span)

    regions(stem_halo // 2, rows // 2, first_step)

    def second_step(i, forward):
        both = conv_pair(hidden, 2 * i + 1, forward, second_w, span)
        total = jnp.zeros((half_span, Q, channels), f32)
        for p, at in enumerate(order(2 * i, forward)):
            value = both[:, p * channels : (p + 1) * channels].reshape(span, Q, channels)
            value = ((stem[at + 2].astype(f32) + value) * half_root).astype(bf16)
            fine[at] = value
            split = value.astype(f32).reshape(half_span, 2, Q, channels)
            total = total + (split[:, 0] + split[:, 1])
        mean = (total * 0.25).astype(bf16)
        pooled[i] = mean
        put_row(cact, i, silu(mean.astype(f32)).reshape(half_span * Q, channels), half_span)

    regions(OUT_HALO // 2, rows // 2, second_step)
    chidden[0] = jnp.zeros(chidden.shape[1:], bf16)
    chidden[chidden.shape[0] - 1] = jnp.zeros(chidden.shape[1:], bf16)

    def cfirst_step(i, forward):
        both = conv_pair(cact, 2 * i, forward, cfirst_w, half_span)
        for p, at in enumerate(order(2 * i, forward)):
            put_row(chidden, at + 1, silu(both[:, p * channels : (p + 1) * channels]), half_span)

    regions(1, rows // 4, cfirst_step)

    def csecond_step(i, forward):
        both = conv_pair(chidden, 2 * i, forward, csecond_w, half_span)
        for p, at in enumerate(order(2 * i, forward)):
            value = both[:, p * channels : (p + 1) * channels].reshape(half_span, Q, channels)
            cout[at] = ((pooled[at + 1].astype(f32) + value) * half_root).astype(bf16)

    regions(1, rows // 4, csecond_step)

    def merge_step(r, carry):
        wide = cout[(r + 3) // 2].astype(f32)[:, None]
        value = fine[r + OUT_HALO - 1].astype(f32).reshape(half_span, 2, Q, channels)
        value = silu((value + wide) * half_root).reshape(span, Q, channels)
        before = pltpu.roll(value[span - 1], 1, 0)[None]
        after = pltpu.roll(value[0], Q - 1, 0)[None]
        value = jnp.concatenate([before, value, after], axis=0).astype(bf16)
        terms[r] = lax.dot_general(
            out_w[...],
            value.reshape((span + 2) * Q, channels),
            (((1,), (1,)), ((), ())),
            preferred_element_type=f32,
        )
        return carry

    lax.fori_loop(0, rows + 2, merge_step, 0)

    def gather_step(r, carry):
        total = None
        for b in range(3):
            part = terms[r, pl.ds(8 * b, 8)]
            for a in range(1, 3):
                part = part + terms[r + a, pl.ds(8 * (3 * a + b), 8)]
            part = part[:, b * Q : b * Q + pixels]
            total = part if total is None else total + part
        rows_out[r] = total
        return carry

    lax.fori_loop(0, rows, gather_step, 0)

    lane = lax.broadcasted_iota(jnp.int32, (pixels, width), 0)
    column = lax.broadcasted_iota(jnp.int32, (pixels, width), 1)
    back = jnp.where((lane % Q) * span + lane // Q == column + COL_HALO, 1.0, 0.0).astype(bf16)
    permuted = rows_out[...].reshape(rows * 8, pixels)
    high = permuted.astype(bf16)
    rest = permuted - high.astype(f32)
    middle = rest.astype(bf16)
    low = (rest - middle.astype(f32)).astype(bf16)
    network = jnp.dot(high, back, preferred_element_type=f32)
    network = network + jnp.dot(middle, back, preferred_element_type=f32)
    network = network + jnp.dot(low, back, preferred_element_type=f32)
    network = jnp.swapaxes(network.reshape(rows, 8, width), 0, 1)[:variables]
    perturbed = pert_ref[...]
    denom = sigma_hat**2 + sigma_data**2
    denoised = sigma_data**2 / denom * perturbed + sigma_hat * sigma_data / math.sqrt(denom) * network
    res_ref[...] = perturbed + (sigma_next - sigma_hat) / sigma_hat * (perturbed - denoised)


def entry(bands, refs):
    band = lax.axis_index("lat")
    kernel(band == 0, band == bands - 1, None, *refs)


def pair_weights(taps):
    low = jnp.pad(taps, ((0, 1), (0, 0), (0, 0), (0, 0)))
    high = jnp.pad(taps, ((1, 0), (0, 0), (0, 0), (0, 0)))
    both = jnp.concatenate([low, high], axis=3)
    return both.reshape(-1, both.shape[3])


def rows_with_halo(own, above, below, across_first, across_last):
    band = lax.axis_index("lat")
    bands = lax.axis_size("lat")
    north = jnp.where(band == 0, jnp.flip(across_first, 1), above)
    south = jnp.where(band == bands - 1, jnp.flip(across_last, 1), below)
    return jnp.concatenate([north, own, south], axis=1)


def across_pole(own, halo):
    sectors = lax.axis_size("lon")
    edges = jnp.concatenate([own[:, :halo], own[:, -halo:]], axis=1)
    got = lax.ppermute(edges, "lon", [(i, (i + sectors // 2) % sectors) for i in range(sectors)])
    return got[:, :halo], got[:, halo:]


def columns_with_halo(own, halo):
    sectors = lax.axis_size("lon")
    up = [(i, (i + 1) % sectors) for i in range(sectors)]
    before = lax.ppermute(own[:, :, -halo:], "lon", up)
    after = lax.ppermute(own[:, :, :halo], "lon", [(j, i) for i, j in up])
    return jnp.concatenate([before, own, after], axis=2)


def body(
    current_sample,
    churn_noise,
    coarse_fields,
    tile_owner,
    input_kernel,
    fine_first,
    fine_second,
    coarse_first,
    coarse_second,
    output_kernel,
):
    band = lax.axis_index("lat")
    bands = lax.axis_size("lat")
    variables, rows, width = current_sample.shape
    channels = fine_first.shape[3]
    span = (width + 2 * COL_HALO) // Q
    pixels = span * Q
    ext_rows = rows + 2 * ROW_HALO
    ins = input_kernel.shape[2]

    perturbed = current_sample + math.sqrt(sigma_hat**2 - sigma_now**2) * churn_noise
    scale_in = 1.0 / math.sqrt(sigma_hat**2 + sigma_data**2)
    noisy = (perturbed * scale_in).astype(bf16)
    up = [(i, i + 1) for i in range(bands - 1)]
    down = [(j, i) for i, j in up]
    above = lax.ppermute(noisy[:, -ROW_HALO:], "lat", up)
    below = lax.ppermute(noisy[:, :ROW_HALO], "lat", down)
    ext = columns_with_halo(rows_with_halo(noisy, above, below, *across_pole(noisy, ROW_HALO)), COL_HALO)

    block_rows = coarse_fields.shape[1]
    gathered = lax.all_gather(coarse_fields.astype(bf16), "lat", axis=1, tiled=True)

    def tile(which):
        slot = tile_owner[jnp.clip(which, 0, bands - 1)]
        return lax.dynamic_slice_in_dim(gathered, slot * block_rows, block_rows, 1)

    own = tile(band)
    cells = rows_with_halo(
        own, tile(band - 1)[:, -CELL_HALO:], tile(band + 1)[:, :CELL_HALO], *across_pole(own, CELL_HALO)
    )
    cells = columns_with_halo(cells, COL_HALO // RATIO)

    ext = jnp.pad(ext.transpose(1, 0, 2), ((0, 0), (0, ins - variables), (0, 0))).reshape(ext_rows * ins, -1)
    cells = cells.transpose(1, 0, 2)
    cells = jnp.pad(cells, ((0, 0), (variables, 0), (0, 128 - cells.shape[2])))
    cells = cells.reshape(-1, 128)
    out_w = jnp.pad(jnp.transpose(output_kernel, (0, 1, 3, 2)), ((0, 0), (0, 0), (0, 8 - variables), (0, 0)))
    out_w = out_w.reshape(-1, channels)

    lanes = -(-(span + 2) * Q // 128) * 128
    half_span = span // 2
    field = lambda n, s: pltpu.VMEM((n, s, Q, channels), bf16)
    fine_rows = rows + 2 * OUT_HALO
    vmem = pl.BlockSpec(memory_space=pltpu.VMEM)

    def call(*refs):
        entry(bands, refs)

    return pl.pallas_call(
        call,
        out_shape=jax.ShapeDtypeStruct(current_sample.shape, f32),
        in_specs=[vmem] * 9,
        out_specs=vmem,
        scratch_shapes=[
            pltpu.VMEM((ext_rows, 3 * ins, lanes), bf16),
            field(ext_rows - 2, span),
            field(ext_rows, span + 2),
            field(ext_rows - 2, span + 2),
            field(fine_rows, span),
            field(fine_rows // 2, half_span),
            field(fine_rows // 2, half_span + 2),
            field(fine_rows // 2, half_span + 2),
            field(fine_rows // 2 - 2, half_span),
            pltpu.VMEM((rows + 2, out_w.shape[0], (span + 2) * Q), f32),
            pltpu.VMEM((rows, 8, pixels), f32),
        ],
        compiler_params=pltpu.CompilerParams(vmem_limit_bytes=56 << 20),
    )(
        ext,
        cells,
        perturbed,
        pair_weights(input_kernel),
        pair_weights(fine_first),
        pair_weights(fine_second),
        pair_weights(coarse_first),
        pair_weights(coarse_second),
        out_w,
    )


def solution(mesh):
    placed = (P(None, "lat", "lon"),) * 3 + (P(),) * 7
    return jax.shard_map(
        body, mesh=mesh, in_specs=placed, out_specs=P(None, "lat", "lon"), check_vma=False
    )
```

```python
import functools
import math

import jax
import jax.numpy as jnp
from jax import lax
from jax.experimental import pallas as pl
from jax.experimental.pallas import tpu as pltpu
from jax.sharding import PartitionSpec as P

RATIO = 8
Q = 16
COL_HALO = 16
OUT_HALO = 6
ROW_HALO = OUT_HALO + 3
CELL_HALO = 2

sigma_now = 1.0
sigma_hat = 1.2
sigma_next = 0.4
sigma_data = 0.5
half_root = math.sqrt(0.5)
f32 = jnp.float32
bf16 = jnp.bfloat16


def silu(v):
    h = 0.5 * v
    return h + h * jnp.tanh(h)


def put_row(ref, row, value, span):
    channels = value.shape[-1]
    value = value.reshape(span, Q, channels)
    ref[row, pl.ds(1, span)] = value.astype(bf16)
    ref[row, 0] = pltpu.roll(value[span - 1], 1, 0).astype(bf16)
    ref[row, span + 1] = pltpu.roll(value[0], Q - 1, 0).astype(bf16)


def conv_pair(src, row, forward, weights, span):
    channels = src.shape[-1]
    parts = []
    for k in range(4):
        at = jnp.where(forward, row + k, row + 3 - k)
        for b in range(3):
            parts.append(src[at, pl.ds(b, span)].reshape(span * Q, channels))
    return jnp.dot(jnp.concatenate(parts, axis=1), weights[...], preferred_element_type=f32)


def kernel(
    north, south, halves_ref, ext_ref, cell_ref, pert_ref, stem_w, first_w, second_w, cfirst_w, csecond_w, out_w,
    res_ref, net, stem, act, hidden, fine, pooled, cact, chidden, cout, terms, rows_out,
):
    del halves_ref
    variables, rows, width = pert_ref.shape
    channels = stem.shape[-1]
    span = stem.shape[1]
    half_span = span // 2
    pixels = span * Q
    lanes = net.shape[-1]
    ext_cols = ext_ref.shape[1]
    ext_rows = rows + 2 * ROW_HALO

    def onehot(depth, cell):
        at = lax.broadcasted_iota(jnp.int32, (depth, lanes), 0)
        lane = lax.broadcasted_iota(jnp.int32, (depth, lanes), 1)
        column = (lane % Q) * span + lane // Q - 1
        inside = (column >= 0) & (column < ext_cols) & (lane < (span + 2) * Q)
        return jnp.where(inside & (at == column // cell), 1.0, 0.0).astype(bf16)

    fine_cols = jnp.dot(ext_ref[...], onehot(ext_cols, 1), preferred_element_type=f32)
    cell_cols = jnp.dot(cell_ref[...], onehot(cell_ref.shape[1], RATIO), preferred_element_type=f32)
    for r in range(ext_rows):
        cell = (r - ROW_HALO + CELL_HALO * RATIO) // RATIO
        both = fine_cols[r * 16 : r * 16 + 16] + cell_cols[cell * 16 : cell * 16 + 16]
        for b in range(3):
            moved = both if b == 0 else pltpu.roll(both, lanes - b * Q, 1)
            net[r, pl.ds(b * 16, 16)] = moved.astype(bf16)

    def regions(halo_pairs, pairs, body):
        def step(i, carry):
            mirrored = (north & (i < halo_pairs)) | (south & (i >= halo_pairs + pairs))
            body(i, jnp.logical_not(mirrored))
            return carry

        lax.fori_loop(0, 2 * halo_pairs + pairs, step, 0)

    def order(row, forward):
        return jnp.where(forward, row, row + 1), jnp.where(forward, row + 1, row)

    stem_halo = ROW_HALO - 1

    def stem_step(i, forward):
        parts = [net[jnp.where(forward, 2 * i + k, 2 * i + 3 - k)][:, :pixels] for k in range(4)]
        both = lax.dot_general(
            jnp.concatenate(parts, axis=0), stem_w[...], (((0,), (0,)), ((), ())), preferred_element_type=f32
        )
        for p, at in enumerate(order(2 * i, forward)):
            value = both[:, p * channels : (p + 1) * channels].astype(bf16)
            stem[at] = value.reshape(span, Q, channels)
            put_row(act, at + 1, silu(value.astype(f32)), span)

    act[0] = jnp.zeros(act.shape[1:], bf16)
    act[ext_rows - 1] = jnp.zeros(act.shape[1:], bf16)
    regions(stem_halo // 2, rows // 2, stem_step)

    def first_step(i, forward):
        both = conv_pair(act, 2 * i, forward, first_w, span)
        for p, at in enumerate(order(2 * i, forward)):
            put_row(hidden, at, silu(both[:, p * channels : (p + 1) * channels]), span)

    regions(stem_halo // 2, rows // 2, first_step)

    def second_step(i, forward):
        both = conv_pair(hidden, 2 * i + 1, forward, second_w, span)
        total = jnp.zeros((half_span, Q, channels), f32)
        for p, at in enumerate(order(2 * i, forward)):
            value = both[:, p * channels : (p + 1) * channels].reshape(span, Q, channels)
            value = ((stem[at + 2].astype(f32) + value) * half_root).astype(bf16)
            fine[at] = value
            split = value.astype(f32).reshape(half_span, 2, Q, channels)
            total = total + (split[:, 0] + split[:, 1])
        mean = (total * 0.25).astype(bf16)
        pooled[i] = mean
        put_row(cact, i, silu(mean.astype(f32)).reshape(half_span * Q, channels), half_span)

    regions(OUT_HALO // 2, rows // 2, second_step)
    chidden[0] = jnp.zeros(chidden.shape[1:], bf16)
    chidden[chidden.shape[0] - 1] = jnp.zeros(chidden.shape[1:], bf16)

    def cfirst_step(i, forward):
        both = conv_pair(cact, 2 * i, forward, cfirst_w, half_span)
        for p, at in enumerate(order(2 * i, forward)):
            put_row(chidden, at + 1, silu(both[:, p * channels : (p + 1) * channels]), half_span)

    regions(1, rows // 4, cfirst_step)

    def csecond_step(i, forward):
        both = conv_pair(chidden, 2 * i, forward, csecond_w, half_span)
        for p, at in enumerate(order(2 * i, forward)):
            value = both[:, p * channels : (p + 1) * channels].reshape(half_span, Q, channels)
            cout[at] = ((pooled[at + 1].astype(f32) + value) * half_root).astype(bf16)

    regions(1, rows // 4, csecond_step)

    def merge_step(r, carry):
        wide = cout[(r + 3) // 2].astype(f32)[:, None]
        value = fine[r + OUT_HALO - 1].astype(f32).reshape(half_span, 2, Q, channels)
        value = silu((value + wide) * half_root).reshape(span, Q, channels)
        before = pltpu.roll(value[span - 1], 1, 0)[None]
        after = pltpu.roll(value[0], Q - 1, 0)[None]
        value = jnp.concatenate([before, value, after], axis=0).astype(bf16)
        terms[r] = lax.dot_general(
            out_w[...],
            value.reshape((span + 2) * Q, channels),
            (((1,), (1,)), ((), ())),
            preferred_element_type=f32,
        )
        return carry

    lax.fori_loop(0, rows + 2, merge_step, 0)

    def gather_step(r, carry):
        total = None
        for b in range(3):
            part = terms[r, pl.ds(8 * b, 8)]
            for a in range(1, 3):
                part = part + terms[r + a, pl.ds(8 * (3 * a + b), 8)]
            part = part[:, b * Q : b * Q + pixels]
            total = part if total is None else total + part
        rows_out[r] = total
        return carry

    lax.fori_loop(0, rows, gather_step, 0)

    lane = lax.broadcasted_iota(jnp.int32, (pixels, width), 0)
    column = lax.broadcasted_iota(jnp.int32, (pixels, width), 1)
    back = jnp.where((lane % Q) * span + lane // Q == column + COL_HALO, 1.0, 0.0).astype(bf16)
    permuted = rows_out[...].reshape(rows * 8, pixels)
    high = permuted.astype(bf16)
    rest = permuted - high.astype(f32)
    middle = rest.astype(bf16)
    low = (rest - middle.astype(f32)).astype(bf16)
    network = jnp.dot(high, back, preferred_element_type=f32)
    network = network + jnp.dot(middle, back, preferred_element_type=f32)
    network = network + jnp.dot(low, back, preferred_element_type=f32)
    network = jnp.swapaxes(network.reshape(rows, 8, width), 0, 1)[:variables]
    perturbed = pert_ref[...]
    denom = sigma_hat**2 + sigma_data**2
    denoised = sigma_data**2 / denom * perturbed + sigma_hat * sigma_data / math.sqrt(denom) * network
    res_ref[...] = perturbed + (sigma_next - sigma_hat) / sigma_hat * (perturbed - denoised)


def entry(bands, refs):
    band = lax.axis_index("lat")
    kernel(band == 0, band == bands - 1, None, *refs)


def pair_weights(taps):
    low = jnp.pad(taps, ((0, 1), (0, 0), (0, 0), (0, 0)))
    high = jnp.pad(taps, ((1, 0), (0, 0), (0, 0), (0, 0)))
    both = jnp.concatenate([low, high], axis=3)
    return both.reshape(-1, both.shape[3])


MESH = pl.DeviceIdType.MESH
LANE = 128
SENT_ROWS = 12


def sector_offsets(sectors):
    half = sectors // 2
    found = []
    for off in (0, 1, -1, half, half + 1, half - 1):
        if off % sectors not in found:
            found.append(off % sectors)
    return found


def exchange_kernel(
    bands, sectors, noisy_ref, tile_ref, ext_ref, tiles_ref, edge, side, tiles, edge_send, edge_recv, side_send,
    side_recv, tile_send, tile_recv,
):
    band, sector = lax.axis_index("lat"), lax.axis_index("lon")
    offsets = sector_offsets(sectors)
    count = len(offsets)
    own_rows, width = noisy_ref.shape
    sent = edge.shape[1]
    others = [(d, k) for d in range(bands) for k in range(count) if d or offsets[k]]

    def peer(d, k):
        return lax.rem(band + d, bands), lax.rem(sector + sectors - offsets[k], sectors)

    barrier = pltpu.get_barrier_semaphore()
    for d, k in others:
        pl.semaphore_signal(barrier, inc=1, device_id=peer(d, k), device_id_type=MESH)
    pl.semaphore_wait(barrier, len(others))

    places = (
        (pl.ds(LANE + width, LANE), pl.ds(0, LANE)),
        (pl.ds(LANE, width), pl.ds(0, width)),
        (pl.ds(0, LANE), pl.ds(width - LANE, LANE)),
    )
    started = []
    arriving = []
    for d, k in others:
        n = d * count + k
        copy = pltpu.make_async_remote_copy(
            src_ref=tile_ref,
            dst_ref=tiles.at[n],
            send_sem=tile_send.at[n],
            recv_sem=tile_recv.at[n],
            device_id=peer(d, k),
            device_id_type=MESH,
        )
        copy.start()
        started.append(copy)
        arriving.append(copy)
    for way, start in enumerate((0, own_rows - sent)):
        polar = band == (0 if way == 0 else bands - 1)
        part = jnp.where(polar, way, 1 - way)
        to_band = jnp.where(polar, band, band + (2 * way - 1))
        turn = jnp.where(polar, sectors // 2, 0)
        for c, (there, here) in enumerate(places):
            target = (to_band, lax.rem(sector + sectors + (c - 1) + turn, sectors))
            copy = pltpu.make_async_remote_copy(
                src_ref=noisy_ref.at[pl.ds(start, sent), here],
                dst_ref=edge.at[part, :, there],
                send_sem=edge_send.at[way, c],
                recv_sem=edge_recv.at[part, c],
                device_id=target,
                device_id_type=MESH,
            )
            copy.start()
            started.append(copy)
            arriving.append(
                pltpu.make_async_remote_copy(
                    src_ref=noisy_ref.at[pl.ds(start, sent), here],
                    dst_ref=edge.at[way, :, there],
                    send_sem=edge_send.at[way, c],
                    recv_sem=edge_recv.at[way, c],
                    device_id=target,
                    device_id_type=MESH,
                )
            )
    for c in (0, 2):
        copy = pltpu.make_async_remote_copy(
            src_ref=noisy_ref.at[:, places[c][1]],
            dst_ref=side.at[1 - c // 2],
            send_sem=side_send.at[c // 2],
            recv_sem=side_recv.at[1 - c // 2],
            device_id=(band, lax.rem(sector + sectors + (c - 1), sectors)),
            device_id_type=MESH,
        )
        copy.start()
        started.append(copy)
        arriving.append(copy)
    ext_ref[pl.ds(sent, own_rows), pl.ds(LANE, width)] = noisy_ref[...]
    for copy in arriving:
        copy.wait_recv()
    for copy in started:
        copy.wait_send()
    ext_ref[pl.ds(sent, own_rows), pl.ds(0, LANE)] = side[0]
    ext_ref[pl.ds(sent, own_rows), pl.ds(LANE + width, LANE)] = side[1]
    ext_ref[pl.ds(0, sent), :] = edge[0]
    ext_ref[pl.ds(sent + own_rows, sent), :] = edge[1]
    for d in range(bands):
        for k in range(count):
            from_band = lax.rem(band + bands - d, bands)
            tiles_ref[from_band, k] = tiles[d * count + k] if d or offsets[k] else tile_ref[...]


def exchange(noisy, tile):
    bands, sectors = lax.axis_size("lat"), lax.axis_size("lon")
    count = len(sector_offsets(sectors))
    variables, rows, width = noisy.shape
    noisy = noisy.transpose(1, 0, 2).reshape(rows * variables, width)
    sent = SENT_ROWS * variables
    wide = width + 2 * LANE
    vmem = pl.BlockSpec(memory_space=pltpu.VMEM)
    dma = pltpu.SemaphoreType.DMA

    def call(*refs):
        exchange_kernel(bands, sectors, *refs)

    ext, tiles = pl.pallas_call(
        call,
        out_shape=(
            jax.ShapeDtypeStruct((rows * variables + 2 * sent, wide), bf16),
            jax.ShapeDtypeStruct((bands, count) + tile.shape, bf16),
        ),
        in_specs=[vmem] * 2,
        out_specs=[vmem] * 2,
        scratch_shapes=[
            pltpu.VMEM((2, sent, wide), bf16),
            pltpu.VMEM((2, rows * variables, LANE), bf16),
            pltpu.VMEM((bands * count,) + tile.shape, bf16),
            dma((2, 3)),
            dma((2, 3)),
            dma((2,)),
            dma((2,)),
            dma((bands * count,)),
            dma((bands * count,)),
        ],
        compiler_params=pltpu.CompilerParams(collective_id=0, has_side_effects=True),
    )(noisy, tile)
    ext = ext.reshape(rows + 2 * SENT_ROWS, variables, wide)
    return ext[:, :, LANE - COL_HALO : LANE + width + COL_HALO], tiles


def body(
    current_sample,
    churn_noise,
    coarse_fields,
    tile_owner,
    input_kernel,
    fine_first,
    fine_second,
    coarse_first,
    coarse_second,
    output_kernel,
):
    band = lax.axis_index("lat")
    bands = lax.axis_size("lat")
    variables, rows, width = current_sample.shape
    channels = fine_first.shape[3]
    span = (width + 2 * COL_HALO) // Q
    pixels = span * Q
    ext_rows = rows + 2 * ROW_HALO
    ins = input_kernel.shape[2]

    perturbed = current_sample + math.sqrt(sigma_hat**2 - sigma_now**2) * churn_noise
    scale_in = 1.0 / math.sqrt(sigma_hat**2 + sigma_data**2)
    noisy = (perturbed * scale_in).astype(bf16)
    block_rows, block_cols = coarse_fields.shape[1:]
    packed = coarse_fields.astype(bf16).reshape(coarse_fields.shape[0], -1)
    packed = jnp.pad(packed, ((variables, ins - variables - packed.shape[0]), (0, 0)))
    got, tiles = exchange(noisy, packed)

    own = got[SENT_ROWS : SENT_ROWS + rows]
    first, last = got[:SENT_ROWS], got[SENT_ROWS + rows :]
    at_north, at_south = band == 0, band == bands - 1
    above = jnp.where(at_north, jnp.flip(first[:ROW_HALO], 0), first[-ROW_HALO:])
    below = jnp.where(at_south, jnp.flip(last[-ROW_HALO:], 0), last[:ROW_HALO])
    ext = jnp.concatenate([above, own, below], axis=0)
    ext = jnp.pad(ext, ((0, 0), (0, ins - variables), (0, 0))).reshape(ext_rows * ins, -1)

    sectors = lax.axis_size("lon")
    offsets = sector_offsets(sectors)
    side_cols = COL_HALO // RATIO

    def block(which, middle):
        slot = tile_owner[jnp.clip(which, 0, bands - 1)]
        all_sectors = lax.dynamic_index_in_dim(tiles, slot, 0, False)

        def at(off):
            return all_sectors[offsets.index(off % sectors)].reshape(ins, block_rows, block_cols)

        return jnp.concatenate(
            [at(middle - 1)[:, :, -side_cols:], at(middle), at(middle + 1)[:, :, :side_cols]], axis=2
        )

    half = sectors // 2
    centre = block(band, 0)
    opposite = block(band, half)
    upper = jnp.where(at_north, jnp.flip(opposite[:, :CELL_HALO], 1), block(band - 1, 0)[:, -CELL_HALO:])
    lower = jnp.where(at_south, jnp.flip(opposite[:, -CELL_HALO:], 1), block(band + 1, 0)[:, :CELL_HALO])
    cells = jnp.concatenate([upper, centre, lower], axis=1).transpose(1, 0, 2)
    cells = jnp.pad(cells, ((0, 0), (0, 0), (0, 128 - cells.shape[2]))).reshape(-1, 128)
    out_w = jnp.pad(jnp.transpose(output_kernel, (0, 1, 3, 2)), ((0, 0), (0, 0), (0, 8 - variables), (0, 0)))
    out_w = out_w.reshape(-1, channels)

    lanes = -(-(span + 2) * Q // 128) * 128
    half_span = span // 2
    field = lambda n, s: pltpu.VMEM((n, s, Q, channels), bf16)
    fine_rows = rows + 2 * OUT_HALO
    vmem = pl.BlockSpec(memory_space=pltpu.VMEM)

    def call(*refs):
        entry(bands, refs)

    return pl.pallas_call(
        call,
        out_shape=jax.ShapeDtypeStruct(current_sample.shape, f32),
        in_specs=[vmem] * 9,
        out_specs=vmem,
        scratch_shapes=[
            pltpu.VMEM((ext_rows, 3 * ins, lanes), bf16),
            field(ext_rows - 2, span),
            field(ext_rows, span + 2),
            field(ext_rows - 2, span + 2),
            field(fine_rows, span),
            field(fine_rows // 2, half_span),
            field(fine_rows // 2, half_span + 2),
            field(fine_rows // 2, half_span + 2),
            field(fine_rows // 2 - 2, half_span),
            pltpu.VMEM((rows + 2, out_w.shape[0], (span + 2) * Q), f32),
            pltpu.VMEM((rows, 8, pixels), f32),
        ],
        compiler_params=pltpu.CompilerParams(vmem_limit_bytes=56 << 20),
    )(
        ext,
        cells,
        perturbed,
        pair_weights(input_kernel),
        pair_weights(fine_first),
        pair_weights(fine_second),
        pair_weights(coarse_first),
        pair_weights(coarse_second),
        out_w,
    )


def solution(mesh):
    placed = (P(None, "lat", "lon"),) * 3 + (P(),) * 7
    return jax.shard_map(
        body, mesh=mesh, in_specs=placed, out_specs=P(None, "lat", "lon"), check_vma=False
    )
```

```python
import functools
import math

import jax
import jax.numpy as jnp
from jax import lax
from jax.experimental import pallas as pl
from jax.experimental.pallas import tpu as pltpu
from jax.sharding import PartitionSpec as P

RATIO = 8
Q = 16
COL_HALO = 16
OUT_HALO = 6
ROW_HALO = OUT_HALO + 3
CELL_HALO = 2

sigma_now = 1.0
sigma_hat = 1.2
sigma_next = 0.4
sigma_data = 0.5
half_root = math.sqrt(0.5)
f32 = jnp.float32
bf16 = jnp.bfloat16


def silu(v):
    h = 0.5 * v
    return h + h * jnp.tanh(h)


def put_row(ref, row, value, span):
    channels = value.shape[-1]
    value = value.reshape(span, Q, channels)
    ref[row, pl.ds(1, span)] = value.astype(bf16)
    ref[row, 0] = pltpu.roll(value[span - 1], 1, 0).astype(bf16)
    ref[row, span + 1] = pltpu.roll(value[0], Q - 1, 0).astype(bf16)


def conv_pair(src, row, forward, weights, span):
    channels = src.shape[-1]
    parts = []
    for k in range(4):
        at = jnp.where(forward, row + k, row + 3 - k)
        for b in range(3):
            parts.append(src[at, pl.ds(b, span)].reshape(span * Q, channels))
    return jnp.dot(jnp.concatenate(parts, axis=1), weights[...], preferred_element_type=f32)


def kernel(
    band, bands, sectors, cell_shape, owner_ref, ext_ref, tiles_ref, pert_ref, stem_k, first_k, second_k, cfirst_k,
    csecond_k, out_k, res_ref, stem_w, first_w, second_w, cfirst_w, csecond_w, net, stem, act, hidden, fine, pooled, cact, chidden, cout, terms, rows_out,
):
    north, south = band == 0, band == bands - 1
    variables, rows, width = pert_ref.shape
    channels = stem.shape[-1]
    span = stem.shape[1]
    half_span = span // 2
    pixels = span * Q
    lanes = net.shape[-1]
    ext_cols = width + 2 * COL_HALO
    ext_rows = rows + 2 * ROW_HALO
    block_rows, block_cols = cell_shape

    def onehot(depth, source, cell):
        at = source(lax.broadcasted_iota(jnp.int32, (depth, lanes), 0))
        lane = lax.broadcasted_iota(jnp.int32, (depth, lanes), 1)
        column = (lane % Q) * span + lane // Q - 1
        inside = (column >= 0) & (column < ext_cols) & (lane < (span + 2) * Q)
        return jnp.where(inside & (at == column // cell), 1.0, 0.0).astype(bf16)

    def cell_source(at):
        packed = tiles_ref.shape[3]
        place = (at // packed - 1) * block_cols + at % packed + COL_HALO // RATIO
        return jnp.where(at % packed < block_cols, place, -1)

    for taps, paired in (
        (stem_k, stem_w),
        (first_k, first_w),
        (second_k, second_w),
        (cfirst_k, cfirst_w),
        (csecond_k, csecond_w),
    ):
        ins = taps.shape[2]
        blank = jnp.zeros((ins, channels), bf16)
        for k in range(4):
            for b in range(3):
                at = pl.ds((3 * k + b) * ins, ins)
                paired[at, pl.ds(0, channels)] = taps[k, b] if k < 3 else blank
                paired[at, pl.ds(channels, channels)] = taps[k - 1, b] if k else blank

    offsets = sector_offsets(sectors)
    packed_cols = tiles_ref.shape[3]
    cells = []
    for j in range(block_rows + 2 * CELL_HALO):
        r = j - CELL_HALO
        if r < 0:
            mirrored, source, plain_row, mirror_row = north, band - 1, block_rows + r, -1 - r
        elif r < block_rows:
            mirrored, source, plain_row, mirror_row = None, band, r, r
        else:
            mirrored, source, plain_row, mirror_row = south, band + 1, r - block_rows, 2 * block_rows - 1 - r
        if mirrored is not None:
            source = jnp.where(mirrored, band, source)
        slot = owner_ref[source]
        parts = []
        for t in (-1, 0, 1):
            here = offsets.index(t % sectors)
            shift = (packed_cols - plain_row * block_cols) % packed_cols
            if mirrored is not None:
                here = jnp.where(mirrored, offsets.index((t + sectors // 2) % sectors), here)
                shift = jnp.where(mirrored, (packed_cols - mirror_row * block_cols) % packed_cols, shift)
            parts.append(pltpu.roll(tiles_ref[slot, here].astype(f32), shift, 1))
        cells.append(jnp.concatenate(parts, axis=1).astype(bf16))
    cells = jnp.concatenate(cells, axis=0)
    cell_cols = jnp.dot(cells, onehot(3 * packed_cols, cell_source, RATIO), preferred_element_type=f32)
    fine_hot = onehot(ext_ref.shape[1], lambda at: at - (LANE - COL_HALO), 1)
    fine_cols = jnp.dot(ext_ref[...], fine_hot, preferred_element_type=f32)

    def fine_row(r):
        return fine_cols[(r + SENT_ROWS) * variables : (r + SENT_ROWS + 1) * variables]

    for i in range(ext_rows):
        r = i - ROW_HALO
        if r < 0:
            value = jnp.where(north, fine_row(-1 - r - SENT_ROWS), fine_row(r))
        elif r < rows:
            value = fine_row(r)
        else:
            value = jnp.where(south, fine_row(rows + SENT_ROWS - 1 - (r - rows)), fine_row(r))
        cell = (r + CELL_HALO * RATIO) // RATIO
        both = jnp.concatenate([value, cell_cols[cell * 16 + variables : cell * 16 + 16]], axis=0)
        for b in range(3):
            moved = both if b == 0 else pltpu.roll(both, lanes - b * Q, 1)
            net[i, pl.ds(b * 16, 16)] = moved.astype(bf16)
    gap = jnp.zeros((8 - variables, channels), f32)
    taps = out_k[...].astype(f32)
    out_w = []
    for t in range(9):
        out_w += [taps[t * variables : (t + 1) * variables], gap]
    out_w = jnp.concatenate(out_w, axis=0).astype(bf16)

    def regions(halo_pairs, pairs, body):
        def step(i, carry):
            mirrored = (north & (i < halo_pairs)) | (south & (i >= halo_pairs + pairs))
            body(i, jnp.logical_not(mirrored))
            return carry

        lax.fori_loop(0, 2 * halo_pairs + pairs, step, 0, unroll=2)

    def order(row, forward):
        return jnp.where(forward, row, row + 1), jnp.where(forward, row + 1, row)

    stem_halo = ROW_HALO - 1

    def stem_step(i, forward):
        parts = [net[jnp.where(forward, 2 * i + k, 2 * i + 3 - k)][:, :pixels] for k in range(4)]
        both = lax.dot_general(
            jnp.concatenate(parts, axis=0), stem_w[...], (((0,), (0,)), ((), ())), preferred_element_type=f32
        )
        for p, at in enumerate(order(2 * i, forward)):
            value = both[:, p * channels : (p + 1) * channels].astype(bf16)
            stem[at] = value.reshape(span, Q, channels)
            put_row(act, at + 1, silu(value.astype(f32)), span)

    act[0] = jnp.zeros(act.shape[1:], bf16)
    act[ext_rows - 1] = jnp.zeros(act.shape[1:], bf16)
    regions(stem_halo // 2, rows // 2, stem_step)

    def first_step(i, forward):
        both = conv_pair(act, 2 * i, forward, first_w, span)
        for p, at in enumerate(order(2 * i, forward)):
            put_row(hidden, at, silu(both[:, p * channels : (p + 1) * channels]), span)

    regions(stem_halo // 2, rows // 2, first_step)

    def second_step(i, forward):
        both = conv_pair(hidden, 2 * i + 1, forward, second_w, span)
        total = jnp.zeros((half_span, Q, channels), f32)
        for p, at in enumerate(order(2 * i, forward)):
            value = both[:, p * channels : (p + 1) * channels].reshape(span, Q, channels)
            value = ((stem[at + 2].astype(f32) + value) * half_root).astype(bf16)
            fine[at] = value
            split = value.astype(f32).reshape(half_span, 2, Q, channels)
            total = total + (split[:, 0] + split[:, 1])
        mean = (total * 0.25).astype(bf16)
        pooled[i] = mean
        put_row(cact, i, silu(mean.astype(f32)).reshape(half_span * Q, channels), half_span)

    regions(OUT_HALO // 2, rows // 2, second_step)
    chidden[0] = jnp.zeros(chidden.shape[1:], bf16)
    chidden[chidden.shape[0] - 1] = jnp.zeros(chidden.shape[1:], bf16)

    def cfirst_step(i, forward):
        both = conv_pair(cact, 2 * i, forward, cfirst_w, half_span)
        for p, at in enumerate(order(2 * i, forward)):
            put_row(chidden, at + 1, silu(both[:, p * channels : (p + 1) * channels]), half_span)

    regions(1, rows // 4, cfirst_step)

    def csecond_step(i, forward):
        both = conv_pair(chidden, 2 * i, forward, csecond_w, half_span)
        for p, at in enumerate(order(2 * i, forward)):
            value = both[:, p * channels : (p + 1) * channels].reshape(half_span, Q, channels)
            cout[at] = ((pooled[at + 1].astype(f32) + value) * half_root).astype(bf16)

    regions(1, rows // 4, csecond_step)

    def merge_step(r, carry):
        wide = cout[(r + 3) // 2].astype(f32)[:, None]
        value = fine[r + OUT_HALO - 1].astype(f32).reshape(half_span, 2, Q, channels)
        value = silu((value + wide) * half_root).reshape(span, Q, channels)
        before = pltpu.roll(value[span - 1], 1, 0)[None]
        after = pltpu.roll(value[0], Q - 1, 0)[None]
        value = jnp.concatenate([before, value, after], axis=0).astype(bf16)
        terms[r] = lax.dot_general(
            out_w,
            value.reshape((span + 2) * Q, channels),
            (((1,), (1,)), ((), ())),
            preferred_element_type=f32,
        )
        return carry

    lax.fori_loop(0, rows + 2, merge_step, 0)

    def gather_step(r, carry):
        total = None
        for b in range(3):
            part = terms[r, pl.ds(8 * b, 8)]
            for a in range(1, 3):
                part = part + terms[r + a, pl.ds(8 * (3 * a + b), 8)]
            part = part[:, b * Q : b * Q + pixels]
            total = part if total is None else total + part
        rows_out[r] = total
        return carry

    lax.fori_loop(0, rows, gather_step, 0)

    lane = lax.broadcasted_iota(jnp.int32, (pixels, width), 0)
    column = lax.broadcasted_iota(jnp.int32, (pixels, width), 1)
    back = jnp.where((lane % Q) * span + lane // Q == column + COL_HALO, 1.0, 0.0).astype(bf16)
    permuted = rows_out[...].reshape(rows * 8, pixels)
    high = permuted.astype(bf16)
    rest = permuted - high.astype(f32)
    middle = rest.astype(bf16)
    low = (rest - middle.astype(f32)).astype(bf16)
    network = jnp.dot(high, back, preferred_element_type=f32)
    network = network + jnp.dot(middle, back, preferred_element_type=f32)
    network = network + jnp.dot(low, back, preferred_element_type=f32)
    network = jnp.swapaxes(network.reshape(rows, 8, width), 0, 1)[:variables]
    perturbed = pert_ref[...]
    denom = sigma_hat**2 + sigma_data**2
    denoised = sigma_data**2 / denom * perturbed + sigma_hat * sigma_data / math.sqrt(denom) * network
    res_ref[...] = perturbed + (sigma_next - sigma_hat) / sigma_hat * (perturbed - denoised)


MESH = pl.DeviceIdType.MESH
LANE = 128
SENT_ROWS = 12


def sector_offsets(sectors):
    half = sectors // 2
    found = []
    for off in (0, 1, -1, half, half + 1, half - 1):
        if off % sectors not in found:
            found.append(off % sectors)
    return found


def exchange_kernel(
    bands, sectors, noisy_ref, tile_ref, ext_ref, tiles_ref, edge, side, tiles, edge_send, edge_recv, side_send,
    side_recv, tile_send, tile_recv,
):
    band, sector = lax.axis_index("lat"), lax.axis_index("lon")
    offsets = sector_offsets(sectors)
    count = len(offsets)
    own_rows, width = noisy_ref.shape
    sent = edge.shape[1]
    others = [(d, k) for d in range(bands) for k in range(count) if d or offsets[k]]

    def peer(d, k):
        return lax.rem(band + d, bands), lax.rem(sector + sectors - offsets[k], sectors)

    barrier = pltpu.get_barrier_semaphore()
    for d, k in others:
        pl.semaphore_signal(barrier, inc=1, device_id=peer(d, k), device_id_type=MESH)
    pl.semaphore_wait(barrier, len(others))

    places = (
        (pl.ds(LANE + width, LANE), pl.ds(0, LANE)),
        (pl.ds(LANE, width), pl.ds(0, width)),
        (pl.ds(0, LANE), pl.ds(width - LANE, LANE)),
    )
    started = []
    arriving = []
    for d, k in others:
        n = d * count + k
        copy = pltpu.make_async_remote_copy(
            src_ref=tile_ref,
            dst_ref=tiles.at[n],
            send_sem=tile_send.at[n],
            recv_sem=tile_recv.at[n],
            device_id=peer(d, k),
            device_id_type=MESH,
        )
        copy.start()
        started.append(copy)
        arriving.append(copy)
    for way, start in enumerate((0, own_rows - sent)):
        polar = band == (0 if way == 0 else bands - 1)
        part = jnp.where(polar, way, 1 - way)
        to_band = jnp.where(polar, band, band + (2 * way - 1))
        turn = jnp.where(polar, sectors // 2, 0)
        for c, (there, here) in enumerate(places):
            target = (to_band, lax.rem(sector + sectors + (c - 1) + turn, sectors))
            copy = pltpu.make_async_remote_copy(
                src_ref=noisy_ref.at[pl.ds(start, sent), here],
                dst_ref=edge.at[part, :, there],
                send_sem=edge_send.at[way, c],
                recv_sem=edge_recv.at[part, c],
                device_id=target,
                device_id_type=MESH,
            )
            copy.start()
            started.append(copy)
            arriving.append(
                pltpu.make_async_remote_copy(
                    src_ref=noisy_ref.at[pl.ds(start, sent), here],
                    dst_ref=edge.at[way, :, there],
                    send_sem=edge_send.at[way, c],
                    recv_sem=edge_recv.at[way, c],
                    device_id=target,
                    device_id_type=MESH,
                )
            )
    for c in (0, 2):
        copy = pltpu.make_async_remote_copy(
            src_ref=noisy_ref.at[:, places[c][1]],
            dst_ref=side.at[1 - c // 2],
            send_sem=side_send.at[c // 2],
            recv_sem=side_recv.at[1 - c // 2],
            device_id=(band, lax.rem(sector + sectors + (c - 1), sectors)),
            device_id_type=MESH,
        )
        copy.start()
        started.append(copy)
        arriving.append(copy)
    ext_ref[pl.ds(sent, own_rows), pl.ds(LANE, width)] = noisy_ref[...]
    for copy in arriving:
        copy.wait_recv()
    for copy in started:
        copy.wait_send()
    ext_ref[pl.ds(sent, own_rows), pl.ds(0, LANE)] = side[0]
    ext_ref[pl.ds(sent, own_rows), pl.ds(LANE + width, LANE)] = side[1]
    ext_ref[pl.ds(0, sent), :] = edge[0]
    ext_ref[pl.ds(sent + own_rows, sent), :] = edge[1]
    for d in range(bands):
        for k in range(count):
            from_band = lax.rem(band + bands - d, bands)
            tiles_ref[from_band, k] = tiles[d * count + k] if d or offsets[k] else tile_ref[...]


def exchange(noisy, tile):
    bands, sectors = lax.axis_size("lat"), lax.axis_size("lon")
    count = len(sector_offsets(sectors))
    variables, rows, width = noisy.shape
    noisy = noisy.transpose(1, 0, 2).reshape(rows * variables, width)
    sent = SENT_ROWS * variables
    wide = width + 2 * LANE
    vmem = pl.BlockSpec(memory_space=pltpu.VMEM)
    dma = pltpu.SemaphoreType.DMA

    def call(*refs):
        exchange_kernel(bands, sectors, *refs)

    ext, tiles = pl.pallas_call(
        call,
        out_shape=(
            jax.ShapeDtypeStruct((rows * variables + 2 * sent, wide), bf16),
            jax.ShapeDtypeStruct((bands, count) + tile.shape, bf16),
        ),
        in_specs=[vmem] * 2,
        out_specs=[vmem] * 2,
        scratch_shapes=[
            pltpu.VMEM((2, sent, wide), bf16),
            pltpu.VMEM((2, rows * variables, LANE), bf16),
            pltpu.VMEM((bands * count,) + tile.shape, bf16),
            dma((2, 3)),
            dma((2, 3)),
            dma((2,)),
            dma((2,)),
            dma((bands * count,)),
            dma((bands * count,)),
        ],
        compiler_params=pltpu.CompilerParams(collective_id=0, has_side_effects=True),
    )(noisy, tile)
    return ext, tiles


def body(
    current_sample,
    churn_noise,
    coarse_fields,
    tile_owner,
    input_kernel,
    fine_first,
    fine_second,
    coarse_first,
    coarse_second,
    output_kernel,
):
    bands = lax.axis_size("lat")
    variables, rows, width = current_sample.shape
    channels = fine_first.shape[3]
    span = (width + 2 * COL_HALO) // Q
    pixels = span * Q
    ext_rows = rows + 2 * ROW_HALO
    ins = input_kernel.shape[2]

    perturbed = current_sample + math.sqrt(sigma_hat**2 - sigma_now**2) * churn_noise
    scale_in = 1.0 / math.sqrt(sigma_hat**2 + sigma_data**2)
    noisy = (perturbed * scale_in).astype(bf16)
    block_rows, block_cols = coarse_fields.shape[1:]
    packed = coarse_fields.astype(bf16).reshape(coarse_fields.shape[0], -1)
    packed = jnp.pad(packed, ((variables, ins - variables - packed.shape[0]), (0, 0)))
    ext, tiles = exchange(noisy, packed)

    sectors = lax.axis_size("lon")
    out_k = jnp.transpose(output_kernel, (0, 1, 3, 2)).reshape(-1, channels)
    lanes = -(-(span + 2) * Q // 128) * 128
    half_span = span // 2
    field = lambda n, s: pltpu.VMEM((n, s, Q, channels), bf16)
    fine_rows = rows + 2 * OUT_HALO
    vmem = pl.BlockSpec(memory_space=pltpu.VMEM)

    def call(*refs):
        kernel(lax.axis_index("lat"), bands, sectors, (block_rows, block_cols), *refs)

    return pl.pallas_call(
        call,
        out_shape=jax.ShapeDtypeStruct(current_sample.shape, f32),
        in_specs=[pl.BlockSpec(memory_space=pltpu.SMEM)] + [vmem] * 9,
        out_specs=vmem,
        scratch_shapes=[
            pltpu.VMEM((12 * ins, 2 * channels), bf16),
            *[pltpu.VMEM((12 * channels, 2 * channels), bf16)] * 4,
            pltpu.VMEM((ext_rows, 3 * ins, lanes), bf16),
            field(ext_rows - 2, span),
            field(ext_rows, span + 2),
            field(ext_rows - 2, span + 2),
            field(fine_rows, span),
            field(fine_rows // 2, half_span),
            field(fine_rows // 2, half_span + 2),
            field(fine_rows // 2, half_span + 2),
            field(fine_rows // 2 - 2, half_span),
            pltpu.VMEM((rows + 2, 72, (span + 2) * Q), f32),
            pltpu.VMEM((rows, 8, pixels), f32),
        ],
        compiler_params=pltpu.CompilerParams(vmem_limit_bytes=56 << 20),
    )(
        tile_owner,
        ext,
        tiles,
        perturbed,
        input_kernel,
        fine_first,
        fine_second,
        coarse_first,
        coarse_second,
        out_k,
    )


def solution(mesh):
    placed = (P(None, "lat", "lon"),) * 3 + (P(),) * 7
    return jax.shard_map(
        body, mesh=mesh, in_specs=placed, out_specs=P(None, "lat", "lon"), check_vma=False
    )
```

```python
import functools
import math

import jax
import jax.numpy as jnp
from jax import lax
from jax.experimental import pallas as pl
from jax.experimental.pallas import tpu as pltpu
from jax.sharding import PartitionSpec as P

RATIO = 8
Q = 16
COL_HALO = 16
OUT_HALO = 6
ROW_HALO = OUT_HALO + 3
CELL_HALO = 2

sigma_now = 1.0
sigma_hat = 1.2
sigma_next = 0.4
sigma_data = 0.5
half_root = math.sqrt(0.5)
f32 = jnp.float32
bf16 = jnp.bfloat16


def silu(v):
    h = 0.5 * v
    return h + h * jnp.tanh(h)


def put_row(ref, row, value, span):
    channels = value.shape[-1]
    value = value.reshape(span, Q, channels)
    ref[row, pl.ds(1, span)] = value.astype(bf16)
    ref[row, 0] = pltpu.roll(value[span - 1], 1, 0).astype(bf16)
    ref[row, span + 1] = pltpu.roll(value[0], Q - 1, 0).astype(bf16)


def conv_pair(src, row, forward, weights, span):
    channels = src.shape[-1]
    parts = []
    for k in range(4):
        at = jnp.where(forward, row + k, row + 3 - k)
        for b in range(3):
            parts.append(src[at, pl.ds(b, span)].reshape(span * Q, channels))
    return jnp.dot(jnp.concatenate(parts, axis=1), weights[...], preferred_element_type=f32)


def kernel(
    band, bands, sectors, cell_shape, owner_ref, ext_ref, tiles_ref, pert_ref, stem_k, first_k, second_k, cfirst_k,
    csecond_k, out_k, res_ref, stem_w, first_w, second_w, cfirst_w, csecond_w, net, stem, act, hidden, fine, pooled, cact, chidden, cout, terms, rows_out,
):
    north, south = band == 0, band == bands - 1
    variables, rows, width = pert_ref.shape
    channels = stem.shape[-1]
    span = stem.shape[1]
    half_span = span // 2
    pixels = span * Q
    lanes = net.shape[-1]
    ext_cols = width + 2 * COL_HALO
    ext_rows = rows + 2 * ROW_HALO
    block_rows, block_cols = cell_shape

    def onehot(depth, source, cell):
        at = source(lax.broadcasted_iota(jnp.int32, (depth, lanes), 0))
        lane = lax.broadcasted_iota(jnp.int32, (depth, lanes), 1)
        column = (lane % Q) * span + lane // Q - 1
        inside = (column >= 0) & (column < ext_cols) & (lane < (span + 2) * Q)
        return jnp.where(inside & (at == column // cell), 1.0, 0.0).astype(bf16)

    def cell_source(at):
        packed = tiles_ref.shape[3]
        place = (at // packed - 1) * block_cols + at % packed + COL_HALO // RATIO
        return jnp.where(at % packed < block_cols, place, -1)

    for taps, paired in (
        (stem_k, stem_w),
        (first_k, first_w),
        (second_k, second_w),
        (cfirst_k, cfirst_w),
        (csecond_k, csecond_w),
    ):
        ins = taps.shape[2]
        blank = jnp.zeros((ins, channels), bf16)
        for k in range(4):
            for b in range(3):
                at = pl.ds((3 * k + b) * ins, ins)
                paired[at, pl.ds(0, channels)] = taps[k, b] if k < 3 else blank
                paired[at, pl.ds(channels, channels)] = taps[k - 1, b] if k else blank

    offsets = sector_offsets(sectors)
    packed_cols = tiles_ref.shape[3]
    cells = []
    for j in range(block_rows + 2 * CELL_HALO):
        r = j - CELL_HALO
        if r < 0:
            mirrored, source, plain_row, mirror_row = north, band - 1, block_rows + r, -1 - r
        elif r < block_rows:
            mirrored, source, plain_row, mirror_row = None, band, r, r
        else:
            mirrored, source, plain_row, mirror_row = south, band + 1, r - block_rows, 2 * block_rows - 1 - r
        if mirrored is not None:
            source = jnp.where(mirrored, band, source)
        slot = owner_ref[source]
        parts = []
        for t in (-1, 0, 1):
            here = offsets.index(t % sectors)
            shift = (packed_cols - plain_row * block_cols) % packed_cols
            if mirrored is not None:
                here = jnp.where(mirrored, offsets.index((t + sectors // 2) % sectors), here)
                shift = jnp.where(mirrored, (packed_cols - mirror_row * block_cols) % packed_cols, shift)
            parts.append(pltpu.roll(tiles_ref[slot, here].astype(f32), shift, 1))
        cells.append(jnp.concatenate(parts, axis=1).astype(bf16))
    cells = jnp.concatenate(cells, axis=0)
    cell_cols = jnp.dot(cells, onehot(3 * packed_cols, cell_source, RATIO), preferred_element_type=f32)
    fine_hot = onehot(ext_ref.shape[1], lambda at: at - (LANE - COL_HALO), 1)
    fine_cols = jnp.dot(ext_ref[...], fine_hot, preferred_element_type=f32)

    def fine_row(r):
        return fine_cols[(r + SENT_ROWS) * variables : (r + SENT_ROWS + 1) * variables]

    for i in range(ext_rows):
        r = i - ROW_HALO
        if r < 0:
            value = jnp.where(north, fine_row(-1 - r - SENT_ROWS), fine_row(r))
        elif r < rows:
            value = fine_row(r)
        else:
            value = jnp.where(south, fine_row(rows + SENT_ROWS - 1 - (r - rows)), fine_row(r))
        cell = (r + CELL_HALO * RATIO) // RATIO
        both = jnp.concatenate([value, cell_cols[cell * 16 + variables : cell * 16 + 16]], axis=0)
        for b in range(3):
            moved = both if b == 0 else pltpu.roll(both, lanes - b * Q, 1)
            net[i, pl.ds(b * 16, 16)] = moved.astype(bf16)
    gap = jnp.zeros((8 - variables, channels), f32)
    taps = out_k[...].astype(f32)
    out_w = []
    for t in range(9):
        out_w += [taps[t * variables : (t + 1) * variables], gap]
    out_w = jnp.concatenate(out_w, axis=0).astype(bf16)

    def regions(halo_pairs, pairs, body):
        def step(i, carry):
            mirrored = (north & (i < halo_pairs)) | (south & (i >= halo_pairs + pairs))
            body(i, jnp.logical_not(mirrored))
            return carry

        lax.fori_loop(0, 2 * halo_pairs + pairs, step, 0, unroll=4)

    def order(row, forward):
        return jnp.where(forward, row, row + 1), jnp.where(forward, row + 1, row)

    stem_halo = ROW_HALO - 1

    def stem_step(i, forward):
        parts = [net[jnp.where(forward, 2 * i + k, 2 * i + 3 - k)][:, :pixels] for k in range(4)]
        both = lax.dot_general(
            jnp.concatenate(parts, axis=0), stem_w[...], (((0,), (0,)), ((), ())), preferred_element_type=f32
        )
        for p, at in enumerate(order(2 * i, forward)):
            value = both[:, p * channels : (p + 1) * channels].astype(bf16)
            stem[at] = value.reshape(span, Q, channels)
            put_row(act, at + 1, silu(value.astype(f32)), span)

    act[0] = jnp.zeros(act.shape[1:], bf16)
    act[ext_rows - 1] = jnp.zeros(act.shape[1:], bf16)
    regions(stem_halo // 2, rows // 2, stem_step)

    def first_step(i, forward):
        both = conv_pair(act, 2 * i, forward, first_w, span)
        for p, at in enumerate(order(2 * i, forward)):
            put_row(hidden, at, silu(both[:, p * channels : (p + 1) * channels]), span)

    regions(stem_halo // 2, rows // 2, first_step)

    def second_step(i, forward):
        both = conv_pair(hidden, 2 * i + 1, forward, second_w, span)
        total = jnp.zeros((half_span, Q, channels), f32)
        for p, at in enumerate(order(2 * i, forward)):
            value = both[:, p * channels : (p + 1) * channels].reshape(span, Q, channels)
            value = ((stem[at + 2].astype(f32) + value) * half_root).astype(bf16)
            fine[at] = value
            split = value.astype(f32).reshape(half_span, 2, Q, channels)
            total = total + (split[:, 0] + split[:, 1])
        mean = (total * 0.25).astype(bf16)
        pooled[i] = mean
        put_row(cact, i, silu(mean.astype(f32)).reshape(half_span * Q, channels), half_span)

    regions(OUT_HALO // 2, rows // 2, second_step)
    chidden[0] = jnp.zeros(chidden.shape[1:], bf16)
    chidden[chidden.shape[0] - 1] = jnp.zeros(chidden.shape[1:], bf16)

    def cfirst_step(i, forward):
        both = conv_pair(cact, 2 * i, forward, cfirst_w, half_span)
        for p, at in enumerate(order(2 * i, forward)):
            put_row(chidden, at + 1, silu(both[:, p * channels : (p + 1) * channels]), half_span)

    regions(1, rows // 4, cfirst_step)

    def csecond_step(i, forward):
        both = conv_pair(chidden, 2 * i, forward, csecond_w, half_span)
        for p, at in enumerate(order(2 * i, forward)):
            value = both[:, p * channels : (p + 1) * channels].reshape(half_span, Q, channels)
            cout[at] = ((pooled[at + 1].astype(f32) + value) * half_root).astype(bf16)

    regions(1, rows // 4, csecond_step)

    def merge_step(r, carry):
        wide = cout[(r + 3) // 2].astype(f32)[:, None]
        value = fine[r + OUT_HALO - 1].astype(f32).reshape(half_span, 2, Q, channels)
        value = silu((value + wide) * half_root).reshape(span, Q, channels)
        before = pltpu.roll(value[span - 1], 1, 0)[None]
        after = pltpu.roll(value[0], Q - 1, 0)[None]
        value = jnp.concatenate([before, value, after], axis=0).astype(bf16)
        terms[r] = lax.dot_general(
            out_w,
            value.reshape((span + 2) * Q, channels),
            (((1,), (1,)), ((), ())),
            preferred_element_type=f32,
        )
        return carry

    lax.fori_loop(0, rows + 2, merge_step, 0, unroll=4)

    def gather_step(r, carry):
        total = None
        for b in range(3):
            part = terms[r, pl.ds(8 * b, 8)]
            for a in range(1, 3):
                part = part + terms[r + a, pl.ds(8 * (3 * a + b), 8)]
            part = part[:, b * Q : b * Q + pixels]
            total = part if total is None else total + part
        rows_out[r] = total
        return carry

    lax.fori_loop(0, rows, gather_step, 0, unroll=4)

    lane = lax.broadcasted_iota(jnp.int32, (pixels, width), 0)
    column = lax.broadcasted_iota(jnp.int32, (pixels, width), 1)
    back = jnp.where((lane % Q) * span + lane // Q == column + COL_HALO, 1.0, 0.0).astype(bf16)
    permuted = rows_out[...].reshape(rows * 8, pixels)
    high = permuted.astype(bf16)
    rest = permuted - high.astype(f32)
    middle = rest.astype(bf16)
    low = (rest - middle.astype(f32)).astype(bf16)
    network = jnp.dot(high, back, preferred_element_type=f32)
    network = network + jnp.dot(middle, back, preferred_element_type=f32)
    network = network + jnp.dot(low, back, preferred_element_type=f32)
    network = jnp.swapaxes(network.reshape(rows, 8, width), 0, 1)[:variables]
    perturbed = pert_ref[...]
    denom = sigma_hat**2 + sigma_data**2
    denoised = sigma_data**2 / denom * perturbed + sigma_hat * sigma_data / math.sqrt(denom) * network
    res_ref[...] = perturbed + (sigma_next - sigma_hat) / sigma_hat * (perturbed - denoised)


MESH = pl.DeviceIdType.MESH
LANE = 128
SENT_ROWS = 12


def sector_offsets(sectors):
    half = sectors // 2
    found = []
    for off in (0, 1, -1, half, half + 1, half - 1):
        if off % sectors not in found:
            found.append(off % sectors)
    return found


def exchange_kernel(
    bands, sectors, noisy_ref, tile_ref, ext_ref, tiles_ref, edge, side, tiles, edge_send, edge_recv, side_send,
    side_recv, tile_send, tile_recv,
):
    band, sector = lax.axis_index("lat"), lax.axis_index("lon")
    offsets = sector_offsets(sectors)
    count = len(offsets)
    own_rows, width = noisy_ref.shape
    sent = edge.shape[1]
    others = [(d, k) for d in range(bands) for k in range(count) if d or offsets[k]]

    def peer(d, k):
        return lax.rem(band + d, bands), lax.rem(sector + sectors - offsets[k], sectors)

    barrier = pltpu.get_barrier_semaphore()
    for d, k in others:
        pl.semaphore_signal(barrier, inc=1, device_id=peer(d, k), device_id_type=MESH)
    pl.semaphore_wait(barrier, len(others))

    places = (
        (pl.ds(LANE + width, LANE), pl.ds(0, LANE)),
        (pl.ds(LANE, width), pl.ds(0, width)),
        (pl.ds(0, LANE), pl.ds(width - LANE, LANE)),
    )
    started = []
    arriving = []
    for d, k in others:
        n = d * count + k
        copy = pltpu.make_async_remote_copy(
            src_ref=tile_ref,
            dst_ref=tiles.at[n],
            send_sem=tile_send.at[n],
            recv_sem=tile_recv.at[n],
            device_id=peer(d, k),
            device_id_type=MESH,
        )
        copy.start()
        started.append(copy)
        arriving.append(copy)
    for way, start in enumerate((0, own_rows - sent)):
        polar = band == (0 if way == 0 else bands - 1)
        part = jnp.where(polar, way, 1 - way)
        to_band = jnp.where(polar, band, band + (2 * way - 1))
        turn = jnp.where(polar, sectors // 2, 0)
        for c, (there, here) in enumerate(places):
            target = (to_band, lax.rem(sector + sectors + (c - 1) + turn, sectors))
            copy = pltpu.make_async_remote_copy(
                src_ref=noisy_ref.at[pl.ds(start, sent), here],
                dst_ref=edge.at[part, :, there],
                send_sem=edge_send.at[way, c],
                recv_sem=edge_recv.at[part, c],
                device_id=target,
                device_id_type=MESH,
            )
            copy.start()
            started.append(copy)
            arriving.append(
                pltpu.make_async_remote_copy(
                    src_ref=noisy_ref.at[pl.ds(start, sent), here],
                    dst_ref=edge.at[way, :, there],
                    send_sem=edge_send.at[way, c],
                    recv_sem=edge_recv.at[way, c],
                    device_id=target,
                    device_id_type=MESH,
                )
            )
    for c in (0, 2):
        copy = pltpu.make_async_remote_copy(
            src_ref=noisy_ref.at[:, places[c][1]],
            dst_ref=side.at[1 - c // 2],
            send_sem=side_send.at[c // 2],
            recv_sem=side_recv.at[1 - c // 2],
            device_id=(band, lax.rem(sector + sectors + (c - 1), sectors)),
            device_id_type=MESH,
        )
        copy.start()
        started.append(copy)
        arriving.append(copy)
    ext_ref[pl.ds(sent, own_rows), pl.ds(LANE, width)] = noisy_ref[...]
    for copy in arriving:
        copy.wait_recv()
    for copy in started:
        copy.wait_send()
    ext_ref[pl.ds(sent, own_rows), pl.ds(0, LANE)] = side[0]
    ext_ref[pl.ds(sent, own_rows), pl.ds(LANE + width, LANE)] = side[1]
    ext_ref[pl.ds(0, sent), :] = edge[0]
    ext_ref[pl.ds(sent + own_rows, sent), :] = edge[1]
    for d in range(bands):
        for k in range(count):
            from_band = lax.rem(band + bands - d, bands)
            tiles_ref[from_band, k] = tiles[d * count + k] if d or offsets[k] else tile_ref[...]


def exchange(noisy, tile):
    bands, sectors = lax.axis_size("lat"), lax.axis_size("lon")
    count = len(sector_offsets(sectors))
    variables, rows, width = noisy.shape
    noisy = noisy.transpose(1, 0, 2).reshape(rows * variables, width)
    sent = SENT_ROWS * variables
    wide = width + 2 * LANE
    vmem = pl.BlockSpec(memory_space=pltpu.VMEM)
    dma = pltpu.SemaphoreType.DMA

    def call(*refs):
        exchange_kernel(bands, sectors, *refs)

    ext, tiles = pl.pallas_call(
        call,
        out_shape=(
            jax.ShapeDtypeStruct((rows * variables + 2 * sent, wide), bf16),
            jax.ShapeDtypeStruct((bands, count) + tile.shape, bf16),
        ),
        in_specs=[vmem] * 2,
        out_specs=[vmem] * 2,
        scratch_shapes=[
            pltpu.VMEM((2, sent, wide), bf16),
            pltpu.VMEM((2, rows * variables, LANE), bf16),
            pltpu.VMEM((bands * count,) + tile.shape, bf16),
            dma((2, 3)),
            dma((2, 3)),
            dma((2,)),
            dma((2,)),
            dma((bands * count,)),
            dma((bands * count,)),
        ],
        compiler_params=pltpu.CompilerParams(collective_id=0, has_side_effects=True),
    )(noisy, tile)
    return ext, tiles


def body(
    current_sample,
    churn_noise,
    coarse_fields,
    tile_owner,
    input_kernel,
    fine_first,
    fine_second,
    coarse_first,
    coarse_second,
    output_kernel,
):
    bands = lax.axis_size("lat")
    variables, rows, width = current_sample.shape
    channels = fine_first.shape[3]
    span = (width + 2 * COL_HALO) // Q
    pixels = span * Q
    ext_rows = rows + 2 * ROW_HALO
    ins = input_kernel.shape[2]

    perturbed = current_sample + math.sqrt(sigma_hat**2 - sigma_now**2) * churn_noise
    scale_in = 1.0 / math.sqrt(sigma_hat**2 + sigma_data**2)
    noisy = (perturbed * scale_in).astype(bf16)
    block_rows, block_cols = coarse_fields.shape[1:]
    packed = coarse_fields.astype(bf16).reshape(coarse_fields.shape[0], -1)
    packed = jnp.pad(packed, ((variables, ins - variables - packed.shape[0]), (0, 0)))
    ext, tiles = exchange(noisy, packed)

    sectors = lax.axis_size("lon")
    out_k = jnp.transpose(output_kernel, (0, 1, 3, 2)).reshape(-1, channels)
    lanes = -(-(span + 2) * Q // 128) * 128
    half_span = span // 2
    field = lambda n, s: pltpu.VMEM((n, s, Q, channels), bf16)
    fine_rows = rows + 2 * OUT_HALO
    vmem = pl.BlockSpec(memory_space=pltpu.VMEM)

    def call(*refs):
        kernel(lax.axis_index("lat"), bands, sectors, (block_rows, block_cols), *refs)

    return pl.pallas_call(
        call,
        out_shape=jax.ShapeDtypeStruct(current_sample.shape, f32),
        in_specs=[pl.BlockSpec(memory_space=pltpu.SMEM)] + [vmem] * 9,
        out_specs=vmem,
        scratch_shapes=[
            pltpu.VMEM((12 * ins, 2 * channels), bf16),
            *[pltpu.VMEM((12 * channels, 2 * channels), bf16)] * 4,
            pltpu.VMEM((ext_rows, 3 * ins, lanes), bf16),
            field(ext_rows - 2, span),
            field(ext_rows, span + 2),
            field(ext_rows - 2, span + 2),
            field(fine_rows, span),
            field(fine_rows // 2, half_span),
            field(fine_rows // 2, half_span + 2),
            field(fine_rows // 2, half_span + 2),
            field(fine_rows // 2 - 2, half_span),
            pltpu.VMEM((rows + 2, 72, (span + 2) * Q), f32),
            pltpu.VMEM((rows, 8, pixels), f32),
        ],
        compiler_params=pltpu.CompilerParams(vmem_limit_bytes=56 << 20),
    )(
        tile_owner,
        ext,
        tiles,
        perturbed,
        input_kernel,
        fine_first,
        fine_second,
        coarse_first,
        coarse_second,
        out_k,
    )


def solution(mesh):
    placed = (P(None, "lat", "lon"),) * 3 + (P(),) * 7
    return jax.shard_map(
        body, mesh=mesh, in_specs=placed, out_specs=P(None, "lat", "lon"), check_vma=False
    )
```
